32 devices in a mesh: row: 4 (over z), col: 8 (over y, x, core).
Axes of the slice: x: 2, y: 2, z: 4, core: 2. Of those that a mesh axis runs over, the one named last changes fastest.
Arguments:
- trail_adjoint: float32 [4096, 4096], P('row', 'col'), may hold values from -0.09375 to 0.09375
- panel: float32 [4096, 128], P('row', 'col')
- panel_adjoint: float32 [4096, 128], P('row', 'col'), may hold values from -6 to 6
- inv_diag: float32 [128, 128], replicated, as said below
- panel_index: int32 [1], replicated, may hold values from 832 to 895
Outputs:
- panel_grad: float32 [4096, 128], P('row', 'col')
- diag_grad: float32 [128, 128], P(None, 'col')
The draws below stay inside these ranges and needn't reach their ends.
Inputs may be any that keep to these rules, and one draw needn't show every extreme that they name: inv_diag is lower triangular with a positive diagonal.
All inputs are finite; a program needn't handle non-finite values.
Results may differ from the reference program's by a relative error of at most 0.000075.
Values sent between devices are 32-bit elements; how exact they have to be, the bound alone decides.
A program may use at most 64 MiB of HBM per device.

```python
import jax
import jax.numpy as jnp
from jax import lax

B = 128
M = 4096
LOC_ROWS = 1024
N_ROW = 4
N_COL = 8


def draw_panel(key, part):
    base_key = jax.random.fold_in(key, 0)
    row_device = (jnp.arange(M) // LOC_ROWS).astype(jnp.float32)
    dev_count = max(M // LOC_ROWS - 1, 1)
    rise_scale = 1.0 + 2.0 * row_device / dev_count
    base_draw = jnp.clip(jax.random.normal(base_key, (M, B), jnp.float32), -4.0, 4.0)
    return (base_draw * rise_scale[:, None] * M ** (-0.25)).astype(jnp.float32)


def draw_inv_diag(key, part):
    first_key, second_key = jax.random.split(key)
    lower_part = 0.5 * jax.random.normal(first_key, (B, B), jnp.float32) / jnp.sqrt(jnp.float32(B))
    diag_values = jnp.exp(jax.random.uniform(second_key, (B,), jnp.float32, jnp.log(0.5), jnp.log(2.0)))
    return (jnp.tril(lower_part, -1) + jnp.diag(diag_values)).astype(jnp.float32)


def level_of(rng, shape, pieces, smallest, top_value):
    gain = 1.0
    for dim, blocks in pieces:
        steps = jax.random.uniform(jax.random.fold_in(jax.random.fold_in(rng, 6), dim), (blocks,), jnp.float32, smallest / len(pieces), top_value / len(pieces))
        gain = gain * jnp.repeat(jnp.exp(steps), shape[dim] // blocks).reshape((-1,) + (1,) * (len(shape) - 1 - dim))
    return gain


def scatter_about(key, dims, deviation, bound, shards=(), kind=jnp.bfloat16):
    level = level_of(key, dims, shards, -0.22, 0.18) if shards else 1.0
    drawn = jax.random.normal(key, dims, jnp.float32) * deviation * level
    return jnp.minimum(jnp.maximum(drawn, -bound), bound).astype(kind)


def setup_inputs(seed: int = 0) -> dict:
    key_of = jax.random.split(jax.random.key(seed), 6)
    trail_adjoint = scatter_about(key_of[0], (M, M), M ** -0.5, 0.09375, ((0, 4), (1, 8)), jnp.float32)
    panel = draw_panel(jax.random.fold_in(key_of[5], 71), 0)
    panel_adjoint = scatter_about(key_of[2], (M, B), 1.0, 6.0, ((0, 4), (1, 8)), jnp.float32)
    inv_diag = draw_inv_diag(jax.random.fold_in(key_of[5], 71), 0)
    panel_index = jax.random.randint(key_of[4], (1,), 832, 896).astype(jnp.int32)
    return {"trail_adjoint": trail_adjoint, "panel": panel, "panel_adjoint": panel_adjoint, "inv_diag": inv_diag, "panel_index": panel_index}


def reference(trail_adjoint, panel, panel_adjoint, inv_diag, panel_index):
    panel_at = panel_index[0]
    block_count = M // B
    blocks_true = jnp.arange(block_count, dtype=jnp.int32)
    row_store = jnp.mod(blocks_true + panel_at + 1, N_ROW).astype(jnp.int32) * (block_count // N_ROW) + blocks_true // N_ROW
    col_store = jnp.mod(blocks_true + panel_at + 1, N_COL).astype(jnp.int32) * (block_count // N_COL) + blocks_true // N_COL
    source = jnp.zeros((block_count,), jnp.int32).at[col_store].set(row_store.astype(jnp.int32))
    panel_blocks = panel.reshape(block_count, B, B)
    column_panel = panel_blocks[source].reshape(M, B)
    product = jnp.dot(trail_adjoint, column_panel, precision=lax.Precision.HIGHEST, preferred_element_type=jnp.float32)
    factor_adjoint = panel_adjoint - 2.0 * product
    panel_grad = jnp.dot(factor_adjoint, inv_diag, precision=lax.Precision.HIGHEST, preferred_element_type=jnp.float32)
    gram = jnp.dot(factor_adjoint.T, panel, precision=lax.Precision.HIGHEST, preferred_element_type=jnp.float32)
    diag_grad = -jnp.dot(inv_diag.T, gram, precision=lax.Precision.HIGHEST, preferred_element_type=jnp.float32)
    return panel_grad, diag_grad
```

```python
import functools

import jax
import jax.numpy as jnp
from jax import lax
from jax.experimental import pallas as pl
from jax.experimental.pallas import tpu as pltpu
from jax.sharding import PartitionSpec as P

MESH = pl.DeviceIdType.MESH


def broadcast(value, axis, root):
    mine = lax.axis_index(axis) == root
    return lax.psum(jnp.where(mine, value, jnp.zeros_like(value)), axis)


def body(trail_adjoint, panel, panel_adjoint, inv_diag, panel_index):
    rows_here, thin_cols = panel.shape
    panel_width = inv_diag.shape[0]
    ways_row = lax.axis_size("row")
    ways_col = lax.axis_size("col")
    ways_ratio = ways_col // ways_row
    col_here = lax.axis_index("col")
    index_k = panel_index[0]
    start_mod = jnp.mod(col_here - index_k - 1, ways_col)
    offset = start_mod // ways_row
    col_blocks = rows_here // (panel_width * ways_ratio)
    root_row = jnp.mod(col_here, ways_row)
    panel_rows = lax.all_gather(panel, "col", axis=1, tiled=True)
    shaped = broadcast(panel_rows, "row", root_row).reshape(
        col_blocks, ways_ratio, panel_width, panel_width
    )
    chosen = lax.dynamic_slice_in_dim(shaped, offset, 1, 1)
    column_panel = chosen.reshape(col_blocks * panel_width, panel_width)
    product = jnp.dot(
        trail_adjoint,
        column_panel,
        precision=lax.Precision.HIGHEST,
        preferred_element_type=jnp.float32,
    )
    placed = lax.dynamic_update_slice_in_dim(
        jnp.zeros((rows_here, panel_width), jnp.float32), panel_adjoint, col_here * thin_cols, 1
    )
    local_term = placed - 2.0 * product
    my_inverse = lax.dynamic_slice_in_dim(inv_diag, col_here * thin_cols, thin_cols, 1)
    contract_rows = (((0,), (0,)), ((), ()))
    thin_part = lax.psum_scatter(local_term, "col", scatter_dimension=1, tiled=True)
    full_rows = lax.all_gather(thin_part, "col", axis=1, tiled=True)
    panel_grad = jnp.dot(
        full_rows, my_inverse, precision=lax.Precision.HIGHEST, preferred_element_type=jnp.float32
    )
    gram_local = lax.dot_general(
        full_rows,
        panel,
        contract_rows,
        precision=lax.Precision.HIGHEST,
        preferred_element_type=jnp.float32,
    )
    gram_total = lax.psum(gram_local, "row")
    diag_grad = -lax.dot_general(
        inv_diag,
        gram_total,
        contract_rows,
        precision=lax.Precision.HIGHEST,
        preferred_element_type=jnp.float32,
    )
    return (panel_grad, diag_grad)


def split(value):
    high = value.astype(jnp.bfloat16)
    return high, (value - high.astype(jnp.float32)).astype(jnp.bfloat16)


def dot(a, b, dims):
    return lax.dot_general(a, b, (dims, ((), ())), preferred_element_type=jnp.float32)


def kernel(
    n_row, n_col, idx_ref, trail_ref, panel_ref, adj_ref, inv_ref, grad_ref, diag_ref,
    trail_v, t_hi, t_lo, base, z_buf, p_full, stage, cp_buf, q_buf, q_in, d_buf, d_in, d_z,
    t_sem, z_send, z_recv, p_send, p_recv, c_send, c_recv, q_send, q_recv, d_send, d_recv, dz_send, dz_recv,
):
    thin, rows = panel_ref.shape
    width = inv_ref.shape[0]
    cols = trail_ref.shape[1]
    ratio = n_col // n_row
    my_row, my_col = lax.axis_index("row"), lax.axis_index("col")

    load = pltpu.make_async_copy(trail_ref, trail_v, t_sem)
    load.start()

    def row_at(shift):
        return {"row": lax.rem(my_row + shift, n_row)}

    def col_at(shift):
        return {"col": lax.rem(my_col + shift, n_col)}

    def col_from(shift):
        return lax.rem(my_col + n_col - shift, n_col)

    barrier = pltpu.get_barrier_semaphore()
    for shift in range(1, n_row):
        pl.semaphore_signal(barrier, inc=1, device_id=row_at(shift), device_id_type=MESH)
    for shift in range(1, n_col):
        pl.semaphore_signal(barrier, inc=1, device_id=col_at(shift), device_id_type=MESH)
    pl.semaphore_wait(barrier, n_row + n_col - 2)

    def remote(src, dst, send, recv, where):
        return pltpu.make_async_remote_copy(
            src_ref=src, dst_ref=dst, send_sem=send, recv_sem=recv, device_id=where, device_id_type=MESH
        )

    z_copies = [
        remote(panel_ref, z_buf.at[s], z_send.at[s], z_recv.at[s], row_at(s)) for s in range(1, n_row)
    ]
    for copy in z_copies:
        copy.start()
    p_copies = [
        remote(panel_ref, p_full.at[my_col], p_send.at[s], p_recv.at[s], col_at(s)) for s in range(1, n_col)
    ]

    index_k = idx_ref[0]

    def forward(shift):
        piece = panel_ref[...] if shift == 0 else z_buf[shift]
        source = lax.rem(my_row + n_row - shift, n_row)
        for group in range(ratio):
            target = source + n_row * group
            offset = jnp.mod(target - index_k - 1, n_col) // n_row
            slot = shift * ratio + group
            for block in range(rows // (width * ratio)):
                at = block * ratio * width
                part = piece[:, at : at + width]
                for other in range(1, ratio):
                    part = jnp.where(
                        offset == other, piece[:, at + other * width : at + (other + 1) * width], part
                    )
                stage[slot, :, block * width : (block + 1) * width] = part
            away = lax.rem(target + n_col - my_col, n_col)

            @pl.when(away != 0)
            def _():
                remote(
                    stage.at[slot], cp_buf.at[my_col], c_send.at[away], c_recv.at[away], {"col": target}
                ).start()

            @pl.when(away == 0)
            def _():
                cp_buf[my_col] = stage[slot]

    forward(0)
    for copy in p_copies:
        copy.start()
    p_full[my_col] = panel_ref[...]

    adj_hi, adj_lo = split(adj_ref[...])
    inv_hi, inv_lo = split(inv_ref[pl.ds(pl.multiple_of(my_col * thin, 8), thin), :])
    base[...] = dot(
        jnp.concatenate([inv_hi, inv_lo, inv_hi], 0), jnp.concatenate([adj_hi, adj_hi, adj_lo], 0), ((0,), (0,))
    )
    load.wait()
    trail_t = trail_v[...].T
    hi, lo = split(trail_t)
    t_hi[...] = hi
    t_lo[...] = lo

    for shift in range(1, n_row):
        z_copies[shift - 1].wait_recv()
        forward(shift)

    inv_hi, inv_lo = split(inv_ref[...].T)
    for s in range(1, n_col):
        where = cp_buf.at[col_from(s)]
        remote(where, where, c_send.at[s], c_recv.at[s], col_at(s)).wait_recv()
    cp_hi, cp_lo = split(cp_buf[...].reshape(width, cols))
    w = -2.0 * dot(
        jnp.concatenate([inv_hi, inv_lo, inv_hi], 1), jnp.concatenate([cp_hi, cp_hi, cp_lo], 0), ((1,), (0,))
    )
    w_hi, w_lo = split(w)
    both = dot(jnp.concatenate([w_hi, w_lo], 0), t_hi[...], ((1,), (0,)))
    q = base[...] + both[:width] + both[width:] + dot(w_hi, t_lo[...], ((1,), (0,)))
    q_buf[...] = q.reshape(n_col, thin, rows)
    q_copies = []
    for s in range(1, n_col):
        copy = remote(
            q_buf.at[lax.rem(my_col + s, n_col)], q_in.at[s], q_send.at[s], q_recv.at[s], col_at(s)
        )
        copy.start()
        q_copies.append(copy)

    for s in range(1, n_col):
        where = p_full.at[col_from(s)]
        remote(where, where, p_send.at[s], p_recv.at[s], col_at(s)).wait_recv()
    q_hi, q_lo = split(q)
    f_hi, f_lo = split(p_full[...].reshape(width, rows))
    nt = ((1,), (1,))
    d = -(dot(f_hi, q_hi, nt) + dot(f_hi, q_lo, nt) + dot(f_lo, q_hi, nt))
    d_buf[...] = d.reshape(n_col, thin, width)
    d_copies = []
    for s in range(1, n_col):
        copy = remote(
            d_buf.at[lax.rem(my_col + s, n_col)], d_in.at[s], d_send.at[s], d_recv.at[s], col_at(s)
        )
        copy.start()
        d_copies.append(copy)
    total = d_buf[my_col]
    for s in range(1, n_col):
        d_copies[s - 1].wait_recv()
        total = total + d_in[s]
    d_z[my_row] = total
    dz_copies = []
    for s in range(1, n_row):
        copy = remote(d_z.at[my_row], d_z.at[my_row], dz_send.at[s], dz_recv.at[s], row_at(s))
        copy.start()
        dz_copies.append(copy)

    total = q_buf[my_col]
    for s in range(1, n_col):
        q_copies[s - 1].wait_recv()
        total = total + q_in[s]
    grad_ref[...] = total

    for s in range(1, n_row):
        where = d_z.at[lax.rem(my_row + n_row - s, n_row)]
        remote(where, where, dz_send.at[s], dz_recv.at[s], row_at(s)).wait_recv()
    total = d_z[0]
    for r in range(1, n_row):
        total = total + d_z[r]
    diag_ref[...] = total

    for s in range(1, n_col):
        remote(stage.at[0], cp_buf.at[my_col], c_send.at[s], c_recv.at[s], col_at(s)).wait_send()
    for copy in z_copies + p_copies + q_copies + d_copies + dz_copies:
        copy.wait_send()


def fused(trail_adjoint, panel, panel_adjoint, inv_diag, panel_index):
    rows, thin = panel.shape
    cols = trail_adjoint.shape[1]
    width = inv_diag.shape[0]
    n_row, n_col = lax.axis_size("row"), lax.axis_size("col")
    f32, bf16 = jnp.float32, jnp.bfloat16
    vmem = pl.BlockSpec(memory_space=pltpu.VMEM)
    dma = pltpu.SemaphoreType.DMA
    grad, diag = pl.pallas_call(
        functools.partial(kernel, n_row, n_col),
        out_shape=(jax.ShapeDtypeStruct((thin, rows), f32), jax.ShapeDtypeStruct((thin, width), f32)),
        in_specs=[pl.BlockSpec(memory_space=pltpu.SMEM), pl.BlockSpec(memory_space=pl.ANY), vmem, vmem, vmem],
        out_specs=(vmem, vmem),
        scratch_shapes=[
            pltpu.VMEM((rows, cols), f32),
            pltpu.VMEM((cols, rows), bf16),
            pltpu.VMEM((cols, rows), bf16),
            pltpu.VMEM((width, rows), f32),
            pltpu.VMEM((n_row, thin, rows), f32),
            pltpu.VMEM((n_col, thin, rows), f32),
            pltpu.VMEM((n_col, thin, cols), f32),
            pltpu.VMEM((n_col, thin, cols), f32),
            pltpu.VMEM((n_col, thin, rows), f32),
            pltpu.VMEM((n_col, thin, rows), f32),
            pltpu.VMEM((n_col, thin, width), f32),
            pltpu.VMEM((n_col, thin, width), f32),
            pltpu.VMEM((n_row, thin, width), f32),
            dma,
            dma((n_row,)), dma((n_row,)),
            dma((n_col,)), dma((n_col,)),
            dma((n_col,)), dma((n_col,)),
            dma((n_col,)), dma((n_col,)),
            dma((n_col,)), dma((n_col,)),
            dma((n_row,)), dma((n_row,)),
        ],
        compiler_params=pltpu.CompilerParams(
            collective_id=0, has_side_effects=True, vmem_limit_bytes=40 * 2**20
        ),
    )(panel_index, trail_adjoint, panel.T, panel_adjoint.T, inv_diag)
    return grad.T, diag.T


def choose(trail_adjoint, panel, panel_adjoint, inv_diag, panel_index):
    step = fused if panel.shape[1] % 8 == 0 else body
    return step(trail_adjoint, panel, panel_adjoint, inv_diag, panel_index)


def solution(mesh):
    in_specs = (P("row", "col"), P("row", "col"), P("row", "col"), P(), P())
    out_specs = (P("row", "col"), P(None, "col"))
    return jax.shard_map(choose, mesh=mesh, in_specs=in_specs, out_specs=out_specs, check_vma=False)
```

```python
import functools

import jax
import jax.numpy as jnp
from jax import lax
from jax.experimental import pallas as pl
from jax.experimental.pallas import tpu as pltpu
from jax.sharding import PartitionSpec as P

MESH = pl.DeviceIdType.MESH


def broadcast(value, axis, root):
    mine = lax.axis_index(axis) == root
    return lax.psum(jnp.where(mine, value, jnp.zeros_like(value)), axis)


def body(trail_adjoint, panel, panel_adjoint, inv_diag, panel_index):
    rows_here, thin_cols = panel.shape
    panel_width = inv_diag.shape[0]
    ways_row = lax.axis_size("row")
    ways_col = lax.axis_size("col")
    ways_ratio = ways_col // ways_row
    col_here = lax.axis_index("col")
    index_k = panel_index[0]
    start_mod = jnp.mod(col_here - index_k - 1, ways_col)
    offset = start_mod // ways_row
    col_blocks = rows_here // (panel_width * ways_ratio)
    root_row = jnp.mod(col_here, ways_row)
    panel_rows = lax.all_gather(panel, "col", axis=1, tiled=True)
    shaped = broadcast(panel_rows, "row", root_row).reshape(
        col_blocks, ways_ratio, panel_width, panel_width
    )
    chosen = lax.dynamic_slice_in_dim(shaped, offset, 1, 1)
    column_panel = chosen.reshape(col_blocks * panel_width, panel_width)
    product = jnp.dot(
        trail_adjoint,
        column_panel,
        precision=lax.Precision.HIGHEST,
        preferred_element_type=jnp.float32,
    )
    placed = lax.dynamic_update_slice_in_dim(
        jnp.zeros((rows_here, panel_width), jnp.float32), panel_adjoint, col_here * thin_cols, 1
    )
    local_term = placed - 2.0 * product
    my_inverse = lax.dynamic_slice_in_dim(inv_diag, col_here * thin_cols, thin_cols, 1)
    contract_rows = (((0,), (0,)), ((), ()))
    thin_part = lax.psum_scatter(local_term, "col", scatter_dimension=1, tiled=True)
    full_rows = lax.all_gather(thin_part, "col", axis=1, tiled=True)
    panel_grad = jnp.dot(
        full_rows, my_inverse, precision=lax.Precision.HIGHEST, preferred_element_type=jnp.float32
    )
    gram_local = lax.dot_general(
        full_rows,
        panel,
        contract_rows,
        precision=lax.Precision.HIGHEST,
        preferred_element_type=jnp.float32,
    )
    gram_total = lax.psum(gram_local, "row")
    diag_grad = -lax.dot_general(
        inv_diag,
        gram_total,
        contract_rows,
        precision=lax.Precision.HIGHEST,
        preferred_element_type=jnp.float32,
    )
    return (panel_grad, diag_grad)


CHUNKS = 2


def split(value):
    high = value.astype(jnp.bfloat16)
    return high, (value - high.astype(jnp.float32)).astype(jnp.bfloat16)


def dot(a, b, dims):
    return lax.dot_general(a, b, (dims, ((), ())), preferred_element_type=jnp.float32)


def kernel(
    n_row, n_col, idx_ref, trail_ref, panel_ref, adj_ref, inv_ref, grad_ref, diag_ref,
    trail_v, panel_v, adj_v, inv_v, t_hi, t_lo, base, z_buf, p_full, stage, cp_buf, q_buf, sib_in, q_sum, q_in,
    d_buf, d_in, d_z, loads, z_send, z_recv, p_send, p_recv, f_send, f_recv, c_send, c_recv, s_send, s_recv,
    q_send, q_recv, d_send, d_recv, dz_send, dz_recv,
):
    thin, rows = panel_v.shape
    width = inv_v.shape[0]
    cols = trail_v.shape[1]
    ratio = n_col // n_row
    n_pair = n_col // 2
    chunks = q_sum.shape[0]
    part = rows // chunks
    my_row, my_col = lax.axis_index("row"), lax.axis_index("col")
    my_pair, my_core = my_col // 2, lax.rem(my_col, 2)
    sibling = {"col": my_pair * 2 + 1 - my_core}

    panel_load = pltpu.make_async_copy(panel_ref, panel_v, loads.at[0])
    inv_load = pltpu.make_async_copy(inv_ref, inv_v, loads.at[1])
    adj_load = pltpu.make_async_copy(adj_ref, adj_v, loads.at[2])
    trail_load = pltpu.make_async_copy(trail_ref, trail_v, loads.at[3])
    for load in (panel_load, inv_load, adj_load, trail_load):
        load.start()

    def row_at(shift):
        return {"row": lax.rem(my_row + shift, n_row)}

    def col_at(shift):
        return {"col": lax.rem(my_col + shift, n_col)}

    def col_from(shift):
        return lax.rem(my_col + n_col - shift, n_col)

    def pair_at(shift):
        return lax.rem(my_pair + shift, n_pair)

    def pair_from(shift):
        return lax.rem(my_pair + n_pair - shift, n_pair)

    barrier = pltpu.get_barrier_semaphore()
    for shift in range(1, n_row):
        pl.semaphore_signal(barrier, inc=1, device_id=row_at(shift), device_id_type=MESH)
    for shift in range(1, n_col):
        pl.semaphore_signal(barrier, inc=1, device_id=col_at(shift), device_id_type=MESH)
    panel_load.wait()
    pl.semaphore_wait(barrier, n_row + n_col - 2)

    def remote(src, dst, send, recv, where):
        return pltpu.make_async_remote_copy(
            src_ref=src, dst_ref=dst, send_sem=send, recv_sem=recv, device_id=where, device_id_type=MESH
        )

    z_copies = [remote(panel_v, z_buf.at[s], z_send.at[s], z_recv.at[s], row_at(s)) for s in range(1, n_row)]
    p_copies = [remote(panel_v, p_full.at[my_col], p_send.at[0], p_recv.at[0], sibling)]
    p_copies += [
        remote(
            panel_v, p_full.at[my_col], p_send.at[s], p_recv.at[s], {"col": pair_at(s) * 2 + my_core}
        )
        for s in range(1, n_pair)
    ]
    for copy in z_copies + p_copies:
        copy.start()

    index_k = idx_ref[0]

    def forward(shift):
        piece = panel_v[...] if shift == 0 else z_buf[shift]
        source = lax.rem(my_row + n_row - shift, n_row)
        for group in range(ratio):
            target = source + n_row * group
            offset = jnp.mod(target - index_k - 1, n_col) // n_row
            slot = shift * ratio + group
            for block in range(rows // (width * ratio)):
                at = block * ratio * width
                chosen = piece[:, at : at + width]
                for other in range(1, ratio):
                    chosen = jnp.where(
                        offset == other, piece[:, at + other * width : at + (other + 1) * width], chosen
                    )
                stage[slot, :, block * width : (block + 1) * width] = chosen
            away = lax.rem(target + n_col - my_col, n_col)

            @pl.when(away != 0)
            def _():
                remote(
                    stage.at[slot], cp_buf.at[my_col], c_send.at[away], c_recv.at[away], {"col": target}
                ).start()

            @pl.when(away == 0)
            def _():
                cp_buf[my_col] = stage[slot]

    forward(0)
    p_full[my_col] = panel_v[...]

    trail_load.wait()
    hi, lo = split(trail_v[...].T)
    t_hi[...] = hi
    t_lo[...] = lo

    relays = []
    for shift in range(1, n_row):
        z_copies[shift - 1].wait_recv()
        forward(shift)
    for s in range(1, n_pair):
        slot = p_full.at[pair_from(s) * 2 + my_core]
        remote(slot, slot, p_send.at[s], p_recv.at[s], sibling).wait_recv()
        relay = remote(slot, slot, f_send.at[s], f_recv.at[s], sibling)
        relay.start()
        relays.append(relay)

    adj_load.wait()
    inv_load.wait()
    adj_hi, adj_lo = split(adj_v[...])
    inv_hi, inv_lo = split(inv_v[pl.ds(pl.multiple_of(my_col * thin, 8), thin), :])
    base[...] = dot(
        jnp.concatenate([inv_hi, inv_lo, inv_hi], 0), jnp.concatenate([adj_hi, adj_hi, adj_lo], 0), ((0,), (0,))
    )
    inv_hi, inv_lo = split(inv_v[...].T)
    for s in range(1, n_col):
        where = cp_buf.at[col_from(s)]
        remote(where, where, c_send.at[s], c_recv.at[s], col_at(s)).wait_recv()
    cp_hi, cp_lo = split(cp_buf[...].reshape(width, cols))
    w = -2.0 * dot(
        jnp.concatenate([inv_hi, inv_lo, inv_hi], 1), jnp.concatenate([cp_hi, cp_hi, cp_lo], 0), ((1,), (0,))
    )
    w_hi, w_lo = split(w)
    w_both = jnp.concatenate([w_hi, w_lo], 0)

    q_parts, s_copies = [], []
    for h in range(chunks):
        at = slice(h * part, (h + 1) * part)
        both = dot(w_both, t_hi[:, at], ((1,), (0,)))
        q = base[:, at] + both[:width] + both[width:] + dot(w_hi, t_lo[:, at], ((1,), (0,)))
        q_parts.append(q)
        by_core = q.reshape(n_pair, 2, thin, part)
        for core in range(2):
            q_buf[h, core] = by_core[:, core]
        copy = remote(q_buf.at[h, 1 - my_core], sib_in.at[h], s_send.at[h], s_recv.at[h], sibling)
        copy.start()
        s_copies.append(copy)

    q_copies = []

    def reduce_out(h):
        s_copies[h].wait_recv()
        q_sum[h] = q_buf[h, my_core] + sib_in[h]
        for s in range(1, n_pair):
            sem = h * n_pair + s
            copy = remote(
                q_sum.at[h, pair_at(s)], q_in.at[h, s], q_send.at[sem], q_recv.at[sem],
                {"col": pair_at(s) * 2 + my_core},
            )
            copy.start()
            q_copies.append(copy)

    reduce_out(0)

    p_copies[0].wait_recv()
    for s in range(1, n_pair):
        slot = p_full.at[pair_from(s) * 2 + 1 - my_core]
        remote(slot, slot, f_send.at[s], f_recv.at[s], sibling).wait_recv()
    d = jnp.zeros((width, width), jnp.float32)
    nt = ((1,), (1,))
    for h in range(chunks):
        q_hi, q_lo = split(q_parts[h])
        f_hi, f_lo = split(p_full[:, :, h * part : (h + 1) * part].reshape(width, part))
        d = d - (dot(f_hi, q_hi, nt) + dot(f_hi, q_lo, nt) + dot(f_lo, q_hi, nt))
    d_buf[...] = d.reshape(n_col, thin, width)
    d_copies = []
    for s in range(1, n_col):
        copy = remote(
            d_buf.at[lax.rem(my_col + s, n_col)], d_in.at[s], d_send.at[s], d_recv.at[s], col_at(s)
        )
        copy.start()
        d_copies.append(copy)
    for h in range(1, chunks):
        reduce_out(h)

    total = d_buf[my_col]
    for s in range(1, n_col):
        d_copies[s - 1].wait_recv()
        total = total + d_in[s]
    d_z[my_row] = total
    dz_copies = []
    for s in range(1, n_row):
        copy = remote(d_z.at[my_row], d_z.at[my_row], dz_send.at[s], dz_recv.at[s], row_at(s))
        copy.start()
        dz_copies.append(copy)

    for h in range(chunks):
        total = q_sum[h, my_pair]
        for s in range(1, n_pair):
            q_copies[h * (n_pair - 1) + s - 1].wait_recv()
            total = total + q_in[h, s]
        grad_ref[:, h * part : (h + 1) * part] = total

    for s in range(1, n_row):
        where = d_z.at[lax.rem(my_row + n_row - s, n_row)]
        remote(where, where, dz_send.at[s], dz_recv.at[s], row_at(s)).wait_recv()
    total = d_z[0]
    for r in range(1, n_row):
        total = total + d_z[r]
    diag_ref[...] = total

    for s in range(1, n_col):
        remote(stage.at[0], cp_buf.at[my_col], c_send.at[s], c_recv.at[s], col_at(s)).wait_send()
    for copy in z_copies + p_copies + relays + s_copies + q_copies + d_copies + dz_copies:
        copy.wait_send()


def fused(trail_adjoint, panel, panel_adjoint, inv_diag, panel_index):
    rows, thin = panel.shape
    cols = trail_adjoint.shape[1]
    width = inv_diag.shape[0]
    n_row, n_col = lax.axis_size("row"), lax.axis_size("col")
    n_pair, chunks = n_col // 2, CHUNKS
    part = rows // chunks
    f32, bf16 = jnp.float32, jnp.bfloat16
    vmem, hbm = pl.BlockSpec(memory_space=pltpu.VMEM), pl.BlockSpec(memory_space=pl.ANY)
    dma = pltpu.SemaphoreType.DMA
    grad, diag = pl.pallas_call(
        functools.partial(kernel, n_row, n_col),
        out_shape=(jax.ShapeDtypeStruct((thin, rows), f32), jax.ShapeDtypeStruct((thin, width), f32)),
        in_specs=[pl.BlockSpec(memory_space=pltpu.SMEM), hbm, hbm, hbm, hbm],
        out_specs=(vmem, vmem),
        scratch_shapes=[
            pltpu.VMEM((rows, cols), f32),
            pltpu.VMEM((thin, rows), f32),
            pltpu.VMEM((thin, rows), f32),
            pltpu.VMEM((width, width), f32),
            pltpu.VMEM((cols, rows), bf16),
            pltpu.VMEM((cols, rows), bf16),
            pltpu.VMEM((width, rows), f32),
            pltpu.VMEM((n_row, thin, rows), f32),
            pltpu.VMEM((n_col, thin, rows), f32),
            pltpu.VMEM((n_col, thin, cols), f32),
            pltpu.VMEM((n_col, thin, cols), f32),
            pltpu.VMEM((chunks, 2, n_pair, thin, part), f32),
            pltpu.VMEM((chunks, n_pair, thin, part), f32),
            pltpu.VMEM((chunks, n_pair, thin, part), f32),
            pltpu.VMEM((chunks, n_pair, thin, part), f32),
            pltpu.VMEM((n_col, thin, width), f32),
            pltpu.VMEM((n_col, thin, width), f32),
            pltpu.VMEM((n_row, thin, width), f32),
            dma((4,)),
            dma((n_row,)), dma((n_row,)),
            dma((n_pair,)), dma((n_pair,)),
            dma((n_pair,)), dma((n_pair,)),
            dma((n_col,)), dma((n_col,)),
            dma((chunks,)), dma((chunks,)),
            dma((chunks * n_pair,)), dma((chunks * n_pair,)),
            dma((n_col,)), dma((n_col,)),
            dma((n_row,)), dma((n_row,)),
        ],
        compiler_params=pltpu.CompilerParams(
            collective_id=0, has_side_effects=True, vmem_limit_bytes=60 * 2**20
        ),
    )(panel_index, trail_adjoint, panel.T, panel_adjoint.T, inv_diag)
    return grad.T, diag.T


def choose(trail_adjoint, panel, panel_adjoint, inv_diag, panel_index):
    step = fused if panel.shape[1] % 8 == 0 else body
    return step(trail_adjoint, panel, panel_adjoint, inv_diag, panel_index)


def solution(mesh):
    in_specs = (P("row", "col"), P("row", "col"), P("row", "col"), P(), P())
    out_specs = (P("row", "col"), P(None, "col"))
    return jax.shard_map(choose, mesh=mesh, in_specs=in_specs, out_specs=out_specs, check_vma=False)
```

```python
import functools

import jax
import jax.numpy as jnp
from jax import lax
from jax.experimental import pallas as pl
from jax.experimental.pallas import tpu as pltpu
from jax.sharding import PartitionSpec as P

MESH = pl.DeviceIdType.MESH


def broadcast(value, axis, root):
    mine = lax.axis_index(axis) == root
    return lax.psum(jnp.where(mine, value, jnp.zeros_like(value)), axis)


def body(trail_adjoint, panel, panel_adjoint, inv_diag, panel_index):
    rows_here, thin_cols = panel.shape
    panel_width = inv_diag.shape[0]
    ways_row = lax.axis_size("row")
    ways_col = lax.axis_size("col")
    ways_ratio = ways_col // ways_row
    col_here = lax.axis_index("col")
    index_k = panel_index[0]
    start_mod = jnp.mod(col_here - index_k - 1, ways_col)
    offset = start_mod // ways_row
    col_blocks = rows_here // (panel_width * ways_ratio)
    root_row = jnp.mod(col_here, ways_row)
    panel_rows = lax.all_gather(panel, "col", axis=1, tiled=True)
    shaped = broadcast(panel_rows, "row", root_row).reshape(
        col_blocks, ways_ratio, panel_width, panel_width
    )
    chosen = lax.dynamic_slice_in_dim(shaped, offset, 1, 1)
    column_panel = chosen.reshape(col_blocks * panel_width, panel_width)
    product = jnp.dot(
        trail_adjoint,
        column_panel,
        precision=lax.Precision.HIGHEST,
        preferred_element_type=jnp.float32,
    )
    placed = lax.dynamic_update_slice_in_dim(
        jnp.zeros((rows_here, panel_width), jnp.float32), panel_adjoint, col_here * thin_cols, 1
    )
    local_term = placed - 2.0 * product
    my_inverse = lax.dynamic_slice_in_dim(inv_diag, col_here * thin_cols, thin_cols, 1)
    contract_rows = (((0,), (0,)), ((), ()))
    thin_part = lax.psum_scatter(local_term, "col", scatter_dimension=1, tiled=True)
    full_rows = lax.all_gather(thin_part, "col", axis=1, tiled=True)
    panel_grad = jnp.dot(
        full_rows, my_inverse, precision=lax.Precision.HIGHEST, preferred_element_type=jnp.float32
    )
    gram_local = lax.dot_general(
        full_rows,
        panel,
        contract_rows,
        precision=lax.Precision.HIGHEST,
        preferred_element_type=jnp.float32,
    )
    gram_total = lax.psum(gram_local, "row")
    diag_grad = -lax.dot_general(
        inv_diag,
        gram_total,
        contract_rows,
        precision=lax.Precision.HIGHEST,
        preferred_element_type=jnp.float32,
    )
    return (panel_grad, diag_grad)


CHUNKS = 2
HALVES = 2


def split(value):
    high = value.astype(jnp.bfloat16)
    return high, (value - high.astype(jnp.float32)).astype(jnp.bfloat16)


def dot(a, b, dims):
    return lax.dot_general(a, b, (dims, ((), ())), preferred_element_type=jnp.float32)


def kernel(
    n_row, n_col, idx_ref, trail_ref, panel_ref, adj_ref, inv_ref, grad_ref, diag_ref,
    trail_v, panel_v, adj_v, inv_v, t_hi, t_lo, base, z_buf, p_full, stage, cp_buf, q_buf, sib_in, q_sum, q_in,
    d_buf, d_in, d_z, loads, z_send, z_recv, p_send, p_recv, f_send, f_recv, c_send, c_recv, s_send, s_recv,
    q_send, q_recv, d_send, d_recv, dz_send, dz_recv,
):
    thin, rows = panel_v.shape
    width = inv_v.shape[0]
    cols = trail_v.shape[1]
    ratio = n_col // n_row
    n_pair = n_col // 2
    chunks = q_sum.shape[0]
    part = rows // chunks
    halves = cp_buf.shape[0]
    half_rows, half_cols = rows // halves, cols // halves
    my_row, my_col = lax.axis_index("row"), lax.axis_index("col")
    my_pair, my_core = my_col // 2, lax.rem(my_col, 2)
    sibling = {"col": my_pair * 2 + 1 - my_core}

    panel_load = pltpu.make_async_copy(panel_ref, panel_v, loads.at[0])
    inv_load = pltpu.make_async_copy(inv_ref, inv_v, loads.at[1])
    adj_load = pltpu.make_async_copy(adj_ref, adj_v, loads.at[2])
    trail_load = pltpu.make_async_copy(trail_ref, trail_v, loads.at[3])
    for load in (panel_load, inv_load, adj_load, trail_load):
        load.start()

    def row_at(shift):
        return {"row": lax.rem(my_row + shift, n_row)}

    def col_at(shift):
        return {"col": lax.rem(my_col + shift, n_col)}

    def col_from(shift):
        return lax.rem(my_col + n_col - shift, n_col)

    def pair_at(mask):
        return my_pair ^ mask

    barrier = pltpu.get_barrier_semaphore()
    for shift in range(1, n_row):
        pl.semaphore_signal(barrier, inc=1, device_id=row_at(shift), device_id_type=MESH)
    for shift in range(1, n_col):
        pl.semaphore_signal(barrier, inc=1, device_id=col_at(shift), device_id_type=MESH)
    panel_load.wait()
    pl.semaphore_wait(barrier, n_row + n_col - 2)

    def remote(src, dst, send, recv, where):
        return pltpu.make_async_remote_copy(
            src_ref=src, dst_ref=dst, send_sem=send, recv_sem=recv, device_id=where, device_id_type=MESH
        )

    def z_copy(s, h):
        lanes, sem = pl.ds(h * half_rows, half_rows), s * halves + h
        return remote(
            panel_v.at[:, lanes], z_buf.at[s, :, lanes], z_send.at[sem], z_recv.at[sem], row_at(s)
        )

    z_copies = [z_copy(s, h) for h in range(halves) for s in range(1, n_row)]
    p_copies = [remote(panel_v, p_full.at[my_col], p_send.at[0], p_recv.at[0], sibling)]
    p_copies += [
        remote(
            panel_v, p_full.at[my_col], p_send.at[s], p_recv.at[s], {"col": pair_at(s) * 2 + my_core}
        )
        for s in range(1, n_pair)
    ]
    for copy in z_copies + p_copies:
        copy.start()

    index_k = idx_ref[0]

    def forward(shift, h):
        lanes = slice(h * half_rows, (h + 1) * half_rows)
        piece = panel_v[:, lanes] if shift == 0 else z_buf[shift, :, lanes]
        source = lax.rem(my_row + n_row - shift, n_row)
        for group in range(ratio):
            target = source + n_row * group
            offset = jnp.mod(target - index_k - 1, n_col) // n_row
            slot = shift * ratio + group
            for block in range(half_rows // (width * ratio)):
                at = block * ratio * width
                chosen = piece[:, at : at + width]
                for other in range(1, ratio):
                    chosen = jnp.where(
                        offset == other, piece[:, at + other * width : at + (other + 1) * width], chosen
                    )
                stage[h, slot, :, block * width : (block + 1) * width] = chosen
            away = lax.rem(target + n_col - my_col, n_col)

            @pl.when(away != 0)
            def _():
                sem = h * n_col + away
                remote(
                    stage.at[h, slot], cp_buf.at[h, my_col], c_send.at[sem], c_recv.at[sem], {"col": target}
                ).start()

            @pl.when(away == 0)
            def _():
                cp_buf[h, my_col] = stage[h, slot]

    for h in range(halves):
        forward(0, h)
    p_full[my_col] = panel_v[...]

    trail_load.wait()
    hi, lo = split(trail_v[...].T)
    t_hi[...] = hi
    t_lo[...] = lo

    relays = []
    for s in range(1, n_pair):
        slot = p_full.at[pair_at(s) * 2 + my_core]
        remote(slot, slot, p_send.at[s], p_recv.at[s], sibling).wait_recv()
        relay = remote(slot, slot, f_send.at[s], f_recv.at[s], sibling)
        relay.start()
        relays.append(relay)

    adj_load.wait()
    inv_load.wait()
    adj_hi, adj_lo = split(adj_v[...])
    inv_hi, inv_lo = split(inv_v[pl.ds(pl.multiple_of(my_col * thin, 8), thin), :])
    base[...] = dot(
        jnp.concatenate([inv_hi, inv_lo, inv_hi], 0), jnp.concatenate([adj_hi, adj_hi, adj_lo], 0), ((0,), (0,))
    )
    inv_hi, inv_lo = split(inv_v[...].T)
    inv_all = jnp.concatenate([inv_hi, inv_lo, inv_hi], 1)

    def forward_all(h):
        for shift in range(1, n_row):
            z_copies[h * (n_row - 1) + shift - 1].wait_recv()
            forward(shift, h)

    for h in range(halves - 1):
        forward_all(h)

    p_copies[0].wait_recv()
    for s in range(1, n_pair):
        slot = p_full.at[pair_at(s) * 2 + 1 - my_core]
        remote(slot, slot, f_send.at[s], f_recv.at[s], sibling).wait_recv()
    nt, nn = ((1,), (1,)), ((1,), (0,))
    f_hi, f_lo = split(p_full[...].reshape(width, rows))
    t_high, t_low = split(trail_v[...])
    x = dot(jnp.concatenate([f_hi, f_lo], 0), t_high, nn)
    x = x[:width] + x[width:] + dot(f_hi, t_low, nn)
    x_hi, x_lo = split(x)
    b_hi, b_lo = split(base[...])
    d = dot(f_hi, b_hi, nt) + dot(f_hi, b_lo, nt) + dot(f_lo, b_hi, nt)

    forward_all(halves - 1)

    def weights(h):
        for s in range(1, n_col):
            where, sem = cp_buf.at[h, col_from(s)], h * n_col + s
            remote(where, where, c_send.at[sem], c_recv.at[sem], col_at(s)).wait_recv()
        cp_hi, cp_lo = split(cp_buf[h].reshape(width, half_cols))
        w = -2.0 * dot(inv_all, jnp.concatenate([cp_hi, cp_hi, cp_lo], 0), nn)
        return split(w)

    def term(w_hi, w_lo, h, at):
        deep = slice(h * half_cols, (h + 1) * half_cols)
        both = dot(jnp.concatenate([w_hi, w_lo], 0), t_hi[deep, at], nn)
        return both[:width] + both[width:] + dot(w_hi, t_lo[deep, at], nn)

    def diag_term(w_hi, w_lo, h):
        deep = slice(h * half_cols, (h + 1) * half_cols)
        x_h, x_l = x_hi[:, deep], x_lo[:, deep]
        return dot(x_h, w_hi, nt) + dot(x_h, w_lo, nt) + dot(x_l, w_hi, nt)

    for half in range(halves - 1):
        w_hi, w_lo = weights(half)
        for h in range(chunks):
            at = slice(h * part, (h + 1) * part)
            base[:, at] += term(w_hi, w_lo, half, at)
        d = d + diag_term(w_hi, w_lo, half)
    w_hi, w_lo = weights(halves - 1)

    s_copies, d_copies = [], []
    for h in range(chunks):
        at = slice(h * part, (h + 1) * part)
        q = base[:, at] + term(w_hi, w_lo, halves - 1, at)
        by_core = q.reshape(n_pair, 2, thin, part)
        for core in range(2):
            q_buf[h, core] = by_core[:, core]
        copy = remote(q_buf.at[h, 1 - my_core], sib_in.at[h], s_send.at[h], s_recv.at[h], sibling)
        copy.start()
        s_copies.append(copy)
        if h == 0:
            d = -(d + diag_term(w_hi, w_lo, halves - 1))
            d_buf[...] = d.reshape(n_col, thin, width)
            for s in range(1, n_col):
                copy = remote(
                    d_buf.at[lax.rem(my_col + s, n_col)], d_in.at[s], d_send.at[s], d_recv.at[s], col_at(s)
                )
                copy.start()
                d_copies.append(copy)

    q_copies = []

    def reduce_out(h):
        s_copies[h].wait_recv()
        q_sum[h] = q_buf[h, my_core] + sib_in[h]
        for s in range(n_pair - 1, 0, -1):
            sem = h * n_pair + s
            copy = remote(
                q_sum.at[h, pair_at(s)], q_in.at[h, s], q_send.at[sem], q_recv.at[sem],
                {"col": pair_at(s) * 2 + my_core},
            )
            copy.start()
            q_copies.append(copy)

    for h in range(chunks):
        reduce_out(h)

    total = d_buf[my_col]
    for s in range(1, n_col):
        d_copies[s - 1].wait_recv()
        total = total + d_in[s]
    d_z[my_row] = total
    dz_copies = []
    for s in range(1, n_row):
        copy = remote(d_z.at[my_row], d_z.at[my_row], dz_send.at[s], dz_recv.at[s], row_at(s))
        copy.start()
        dz_copies.append(copy)

    for h in range(chunks):
        total = q_sum[h, my_pair]
        for s in range(n_pair - 1, 0, -1):
            q_copies[h * (n_pair - 1) + n_pair - 1 - s].wait_recv()
            total = total + q_in[h, s]
        grad_ref[:, h * part : (h + 1) * part] = total

    for s in range(1, n_row):
        where = d_z.at[lax.rem(my_row + n_row - s, n_row)]
        remote(where, where, dz_send.at[s], dz_recv.at[s], row_at(s)).wait_recv()
    total = d_z[0]
    for r in range(1, n_row):
        total = total + d_z[r]
    diag_ref[...] = total

    for h in range(halves):
        for s in range(1, n_col):
            sem = h * n_col + s
            remote(
                stage.at[h, 0], cp_buf.at[h, my_col], c_send.at[sem], c_recv.at[sem], col_at(s)
            ).wait_send()
    for copy in z_copies + p_copies + relays + s_copies + q_copies + d_copies + dz_copies:
        copy.wait_send()


def fused(trail_adjoint, panel, panel_adjoint, inv_diag, panel_index):
    rows, thin = panel.shape
    cols = trail_adjoint.shape[1]
    width = inv_diag.shape[0]
    n_row, n_col = lax.axis_size("row"), lax.axis_size("col")
    n_pair, chunks, halves = n_col // 2, CHUNKS, HALVES
    part = rows // chunks
    f32, bf16 = jnp.float32, jnp.bfloat16
    vmem, hbm = pl.BlockSpec(memory_space=pltpu.VMEM), pl.BlockSpec(memory_space=pl.ANY)
    dma = pltpu.SemaphoreType.DMA
    grad, diag = pl.pallas_call(
        functools.partial(kernel, n_row, n_col),
        out_shape=(pltpu.VMEM((thin, rows), f32), pltpu.VMEM((thin, width), f32)),
        in_specs=[pl.BlockSpec(memory_space=pltpu.SMEM), hbm, hbm, hbm, hbm],
        out_specs=(vmem, vmem),
        scratch_shapes=[
            pltpu.VMEM((rows, cols), f32),
            pltpu.VMEM((thin, rows), f32),
            pltpu.VMEM((thin, rows), f32),
            pltpu.VMEM((width, width), f32),
            pltpu.VMEM((cols, rows), bf16),
            pltpu.VMEM((cols, rows), bf16),
            pltpu.VMEM((width, rows), f32),
            pltpu.VMEM((n_row, thin, rows), f32),
            pltpu.VMEM((n_col, thin, rows), f32),
            pltpu.VMEM((halves, n_col, thin, cols // halves), f32),
            pltpu.VMEM((halves, n_col, thin, cols // halves), f32),
            pltpu.VMEM((chunks, 2, n_pair, thin, part), f32),
            pltpu.VMEM((chunks, n_pair, thin, part), f32),
            pltpu.VMEM((chunks, n_pair, thin, part), f32),
            pltpu.VMEM((chunks, n_pair, thin, part), f32),
            pltpu.VMEM((n_col, thin, width), f32),
            pltpu.VMEM((n_col, thin, width), f32),
            pltpu.VMEM((n_row, thin, width), f32),
            dma((4,)),
            dma((n_row * halves,)), dma((n_row * halves,)),
            dma((n_pair,)), dma((n_pair,)),
            dma((n_pair,)), dma((n_pair,)),
            dma((n_col * halves,)), dma((n_col * halves,)),
            dma((chunks,)), dma((chunks,)),
            dma((chunks * n_pair,)), dma((chunks * n_pair,)),
            dma((n_col,)), dma((n_col,)),
            dma((n_row,)), dma((n_row,)),
        ],
        compiler_params=pltpu.CompilerParams(
            collective_id=0, has_side_effects=True, vmem_limit_bytes=60 * 2**20
        ),
    )(panel_index, trail_adjoint, panel.T, panel_adjoint.T, inv_diag)
    return grad.T, diag.T


def choose(trail_adjoint, panel, panel_adjoint, inv_diag, panel_index):
    step = fused if panel.shape[1] % 8 == 0 else body
    return step(trail_adjoint, panel, panel_adjoint, inv_diag, panel_index)


def solution(mesh):
    in_specs = (P("row", "col"), P("row", "col"), P("row", "col"), P(), P())
    out_specs = (P("row", "col"), P(None, "col"))
    return jax.shard_map(choose, mesh=mesh, in_specs=in_specs, out_specs=out_specs, check_vma=False)
```

```python
import functools

import jax
import jax.numpy as jnp
from jax import lax
from jax.experimental import pallas as pl
from jax.experimental.pallas import tpu as pltpu
from jax.sharding import PartitionSpec as P

MESH = pl.DeviceIdType.MESH


def broadcast(value, axis, root):
    mine = lax.axis_index(axis) == root
    return lax.psum(jnp.where(mine, value, jnp.zeros_like(value)), axis)


def body(trail_adjoint, panel, panel_adjoint, inv_diag, panel_index):
    rows_here, thin_cols = panel.shape
    panel_width = inv_diag.shape[0]
    ways_row = lax.axis_size("row")
    ways_col = lax.axis_size("col")
    ways_ratio = ways_col // ways_row
    col_here = lax.axis_index("col")
    index_k = panel_index[0]
    start_mod = jnp.mod(col_here - index_k - 1, ways_col)
    offset = start_mod // ways_row
    col_blocks = rows_here // (panel_width * ways_ratio)
    root_row = jnp.mod(col_here, ways_row)
    panel_rows = lax.all_gather(panel, "col", axis=1, tiled=True)
    shaped = broadcast(panel_rows, "row", root_row).reshape(
        col_blocks, ways_ratio, panel_width, panel_width
    )
    chosen = lax.dynamic_slice_in_dim(shaped, offset, 1, 1)
    column_panel = chosen.reshape(col_blocks * panel_width, panel_width)
    product = jnp.dot(
        trail_adjoint,
        column_panel,
        precision=lax.Precision.HIGHEST,
        preferred_element_type=jnp.float32,
    )
    placed = lax.dynamic_update_slice_in_dim(
        jnp.zeros((rows_here, panel_width), jnp.float32), panel_adjoint, col_here * thin_cols, 1
    )
    local_term = placed - 2.0 * product
    my_inverse = lax.dynamic_slice_in_dim(inv_diag, col_here * thin_cols, thin_cols, 1)
    contract_rows = (((0,), (0,)), ((), ()))
    thin_part = lax.psum_scatter(local_term, "col", scatter_dimension=1, tiled=True)
    full_rows = lax.all_gather(thin_part, "col", axis=1, tiled=True)
    panel_grad = jnp.dot(
        full_rows, my_inverse, precision=lax.Precision.HIGHEST, preferred_element_type=jnp.float32
    )
    gram_local = lax.dot_general(
        full_rows,
        panel,
        contract_rows,
        precision=lax.Precision.HIGHEST,
        preferred_element_type=jnp.float32,
    )
    gram_total = lax.psum(gram_local, "row")
    diag_grad = -lax.dot_general(
        inv_diag,
        gram_total,
        contract_rows,
        precision=lax.Precision.HIGHEST,
        preferred_element_type=jnp.float32,
    )
    return (panel_grad, diag_grad)


CHUNKS = 2
HALVES = 2


def split(value):
    high = value.astype(jnp.bfloat16)
    return high, (value - high.astype(jnp.float32)).astype(jnp.bfloat16)


def dot(a, b, dims):
    return lax.dot_general(a, b, (dims, ((), ())), preferred_element_type=jnp.float32)


def kernel(
    n_row, n_col, idx_ref, trail_ref, panel_ref, adj_ref, inv_ref, grad_ref, diag_ref,
    trail_v, panel_v, adj_v, inv_v, t_hi, t_lo, base, z_buf, p_full, stage, cp_buf, q_buf, sib_in, q_sum, q_in,
    d_buf, d_in, d_z, loads, z_send, z_recv, p_send, p_recv, f_send, f_recv, c_send, c_recv, s_send, s_recv,
    q_send, q_recv, d_send, d_recv, dz_send, dz_recv,
):
    thin, rows = panel_v.shape
    width = inv_v.shape[0]
    cols = trail_v.shape[1]
    ratio = n_col // n_row
    n_pair = n_col // 2
    chunks = q_sum.shape[0]
    part = rows // chunks
    halves = cp_buf.shape[0]
    half_rows, half_cols = rows // halves, cols // halves
    my_row, my_col = lax.axis_index("row"), lax.axis_index("col")
    my_pair, my_core = my_col // 2, lax.rem(my_col, 2)
    sibling = {"col": my_pair * 2 + 1 - my_core}

    panel_load = pltpu.make_async_copy(panel_ref, panel_v, loads.at[0])
    inv_load = pltpu.make_async_copy(inv_ref, inv_v, loads.at[1])
    adj_load = pltpu.make_async_copy(adj_ref, adj_v, loads.at[2])
    trail_load = pltpu.make_async_copy(trail_ref, trail_v, loads.at[3])
    for load in (panel_load, inv_load, adj_load, trail_load):
        load.start()

    def row_at(shift):
        return {"row": lax.rem(my_row + shift, n_row)}

    def col_at(shift):
        return {"col": lax.rem(my_col + shift, n_col)}

    def col_from(shift):
        return lax.rem(my_col + n_col - shift, n_col)

    def pair_at(mask):
        return my_pair ^ mask

    barrier = pltpu.get_barrier_semaphore()
    for shift in range(1, n_row):
        pl.semaphore_signal(barrier, inc=1, device_id=row_at(shift), device_id_type=MESH)
    for shift in range(1, n_col):
        pl.semaphore_signal(barrier, inc=1, device_id=col_at(shift), device_id_type=MESH)
    panel_load.wait()
    pl.semaphore_wait(barrier, n_row + n_col - 2)

    def remote(src, dst, send, recv, where):
        return pltpu.make_async_remote_copy(
            src_ref=src, dst_ref=dst, send_sem=send, recv_sem=recv, device_id=where, device_id_type=MESH
        )

    def z_copy(source, h, step):
        lanes, sem = pl.ds(h * half_rows, half_rows), source * halves + h
        sends = z_send.at[(step + 1) // 2 * n_row * halves + sem]
        slot = z_buf.at[source, :, lanes]
        return remote(slot, slot, sends, z_recv.at[sem], {"row": jnp.clip(my_row + step, 0, n_row - 1)})

    def has_next(step):
        return my_row < n_row - 1 if step > 0 else my_row > 0

    def pass_on(source, h, step, do):
        @pl.when(has_next(step))
        def _():
            do(z_copy(source, h, step))

    def from_behind(distance, step, do):
        source = my_row - distance * step

        @pl.when(source >= 0 if step > 0 else source < n_row)
        def _():
            do(source)

    z_buf[my_row] = panel_v[...]
    for h in range(halves):
        for step in (1, -1):
            pass_on(my_row, h, step, lambda copy: copy.start())
    p_copies = [remote(panel_v, p_full.at[my_col], p_send.at[0], p_recv.at[0], sibling)]
    p_copies += [
        remote(
            panel_v, p_full.at[my_col], p_send.at[s], p_recv.at[s], {"col": pair_at(s) * 2 + my_core}
        )
        for s in range(1, n_pair)
    ]
    for copy in p_copies:
        copy.start()

    index_k = idx_ref[0]

    def forward(source, h):
        lanes = slice(h * half_rows, (h + 1) * half_rows)
        piece = z_buf[source, :, lanes]
        for group in range(ratio):
            target = source + n_row * group
            offset = jnp.mod(target - index_k - 1, n_col) // n_row
            slot = source * ratio + group
            for block in range(half_rows // (width * ratio)):
                at = block * ratio * width
                chosen = piece[:, at : at + width]
                for other in range(1, ratio):
                    chosen = jnp.where(
                        offset == other, piece[:, at + other * width : at + (other + 1) * width], chosen
                    )
                stage[h, slot, :, block * width : (block + 1) * width] = chosen
            away = lax.rem(target + n_col - my_col, n_col)

            @pl.when(away != 0)
            def _():
                sem = h * n_col + away
                remote(
                    stage.at[h, slot], cp_buf.at[h, my_col], c_send.at[sem], c_recv.at[sem], {"col": target}
                ).start()

            @pl.when(away == 0)
            def _():
                cp_buf[h, my_col] = stage[h, slot]

    for h in range(halves):
        forward(my_row, h)
    p_full[my_col] = panel_v[...]

    trail_load.wait()
    hi, lo = split(trail_v[...].T)
    t_hi[...] = hi
    t_lo[...] = lo

    def hop(distance):
        for h in range(halves):
            for step in (1, -1):

                def receive(source, h=h, step=step):
                    z_copy(source, h, step).wait_recv()
                    pass_on(source, h, step, lambda copy: copy.start())
                    forward(source, h)

                from_behind(distance, step, receive)

    hop(1)
    relays = []
    for s in range(1, n_pair):
        slot = p_full.at[pair_at(s) * 2 + my_core]
        remote(slot, slot, p_send.at[s], p_recv.at[s], sibling).wait_recv()
        relay = remote(slot, slot, f_send.at[s], f_recv.at[s], sibling)
        relay.start()
        relays.append(relay)

    adj_load.wait()
    inv_load.wait()
    adj_hi, adj_lo = split(adj_v[...])
    inv_hi, inv_lo = split(inv_v[pl.ds(pl.multiple_of(my_col * thin, 8), thin), :])
    base[...] = dot(
        jnp.concatenate([inv_hi, inv_lo, inv_hi], 0), jnp.concatenate([adj_hi, adj_hi, adj_lo], 0), ((0,), (0,))
    )
    inv_hi, inv_lo = split(inv_v[...].T)
    inv_all = jnp.concatenate([inv_hi, inv_lo, inv_hi], 1)

    hop(2)

    p_copies[0].wait_recv()
    for s in range(1, n_pair):
        slot = p_full.at[pair_at(s) * 2 + 1 - my_core]
        remote(slot, slot, f_send.at[s], f_recv.at[s], sibling).wait_recv()
    nt, nn = ((1,), (1,)), ((1,), (0,))
    f_hi, f_lo = split(p_full[...].reshape(width, rows))
    t_high, t_low = split(trail_v[...])
    x = dot(jnp.concatenate([f_hi, f_lo], 0), t_high, nn)
    x = x[:width] + x[width:] + dot(f_hi, t_low, nn)
    x_hi, x_lo = split(x)
    b_hi, b_lo = split(base[...])
    d = dot(f_hi, b_hi, nt) + dot(f_hi, b_lo, nt) + dot(f_lo, b_hi, nt)

    for distance in range(3, n_row):
        hop(distance)

    def weights(h):
        for s in range(1, n_col):
            where, sem = cp_buf.at[h, col_from(s)], h * n_col + s
            remote(where, where, c_send.at[sem], c_recv.at[sem], col_at(s)).wait_recv()
        cp_hi, cp_lo = split(cp_buf[h].reshape(width, half_cols))
        w = -2.0 * dot(inv_all, jnp.concatenate([cp_hi, cp_hi, cp_lo], 0), nn)
        return split(w)

    def term(w_hi, w_lo, h, at):
        deep = slice(h * half_cols, (h + 1) * half_cols)
        both = dot(jnp.concatenate([w_hi, w_lo], 0), t_hi[deep, at], nn)
        return both[:width] + both[width:] + dot(w_hi, t_lo[deep, at], nn)

    def diag_term(w_hi, w_lo, h):
        deep = slice(h * half_cols, (h + 1) * half_cols)
        x_h, x_l = x_hi[:, deep], x_lo[:, deep]
        return dot(x_h, w_hi, nt) + dot(x_h, w_lo, nt) + dot(x_l, w_hi, nt)

    for half in range(halves - 1):
        w_hi, w_lo = weights(half)
        for h in range(chunks):
            at = slice(h * part, (h + 1) * part)
            base[:, at] += term(w_hi, w_lo, half, at)
        d = d + diag_term(w_hi, w_lo, half)
    w_hi, w_lo = weights(halves - 1)

    s_copies, d_copies = [], []
    for h in range(chunks):
        at = slice(h * part, (h + 1) * part)
        q = base[:, at] + term(w_hi, w_lo, halves - 1, at)
        by_core = q.reshape(n_pair, 2, thin, part)
        for core in range(2):
            q_buf[h, core] = by_core[:, core]
        copy = remote(q_buf.at[h, 1 - my_core], sib_in.at[h], s_send.at[h], s_recv.at[h], sibling)
        copy.start()
        s_copies.append(copy)
        if h == 0:
            d = -(d + diag_term(w_hi, w_lo, halves - 1))
            d_buf[...] = d.reshape(n_col, thin, width)
            for s in range(1, n_col):
                copy = remote(
                    d_buf.at[lax.rem(my_col + s, n_col)], d_in.at[s], d_send.at[s], d_recv.at[s], col_at(s)
                )
                copy.start()
                d_copies.append(copy)

    q_copies = []

    def reduce_out(h):
        s_copies[h].wait_recv()
        q_sum[h] = q_buf[h, my_core] + sib_in[h]
        for s in range(n_pair - 1, 0, -1):
            sem = h * n_pair + s
            copy = remote(
                q_sum.at[h, pair_at(s)], q_in.at[h, s], q_send.at[sem], q_recv.at[sem],
                {"col": pair_at(s) * 2 + my_core},
            )
            copy.start()
            q_copies.append(copy)

    for h in range(chunks):
        reduce_out(h)

    total = d_buf[my_col]
    for s in range(1, n_col):
        d_copies[s - 1].wait_recv()
        total = total + d_in[s]
    d_z[my_row] = total
    dz_copies = []
    for s in range(1, n_row):
        copy = remote(d_z.at[my_row], d_z.at[my_row], dz_send.at[s], dz_recv.at[s], row_at(s))
        copy.start()
        dz_copies.append(copy)

    for h in range(chunks):
        total = q_sum[h, my_pair]
        for s in range(n_pair - 1, 0, -1):
            q_copies[h * (n_pair - 1) + n_pair - 1 - s].wait_recv()
            total = total + q_in[h, s]
        grad_ref[:, h * part : (h + 1) * part] = total

    for s in range(1, n_row):
        where = d_z.at[lax.rem(my_row + n_row - s, n_row)]
        remote(where, where, dz_send.at[s], dz_recv.at[s], row_at(s)).wait_recv()
    total = d_z[0]
    for r in range(1, n_row):
        total = total + d_z[r]
    diag_ref[...] = total

    for h in range(halves):
        for s in range(1, n_col):
            sem = h * n_col + s
            remote(
                stage.at[h, 0], cp_buf.at[h, my_col], c_send.at[sem], c_recv.at[sem], col_at(s)
            ).wait_send()
    for h in range(halves):
        for step in (1, -1):
            for distance in range(n_row):
                from_behind(
                    distance, step, lambda source: pass_on(source, h, step, lambda copy: copy.wait_send())
                )
    for copy in p_copies + relays + s_copies + q_copies + d_copies + dz_copies:
        copy.wait_send()


def fused(trail_adjoint, panel, panel_adjoint, inv_diag, panel_index):
    rows, thin = panel.shape
    cols = trail_adjoint.shape[1]
    width = inv_diag.shape[0]
    n_row, n_col = lax.axis_size("row"), lax.axis_size("col")
    n_pair, chunks, halves = n_col // 2, CHUNKS, HALVES
    part = rows // chunks
    f32, bf16 = jnp.float32, jnp.bfloat16
    vmem, hbm = pl.BlockSpec(memory_space=pltpu.VMEM), pl.BlockSpec(memory_space=pl.ANY)
    dma = pltpu.SemaphoreType.DMA
    grad, diag = pl.pallas_call(
        functools.partial(kernel, n_row, n_col),
        out_shape=(pltpu.VMEM((thin, rows), f32), pltpu.VMEM((thin, width), f32)),
        in_specs=[pl.BlockSpec(memory_space=pltpu.SMEM), hbm, hbm, hbm, hbm],
        out_specs=(vmem, vmem),
        scratch_shapes=[
            pltpu.VMEM((rows, cols), f32),
            pltpu.VMEM((thin, rows), f32),
            pltpu.VMEM((thin, rows), f32),
            pltpu.VMEM((width, width), f32),
            pltpu.VMEM((cols, rows), bf16),
            pltpu.VMEM((cols, rows), bf16),
            pltpu.VMEM((width, rows), f32),
            pltpu.VMEM((n_row, thin, rows), f32),
            pltpu.VMEM((n_col, thin, rows), f32),
            pltpu.VMEM((halves, n_col, thin, cols // halves), f32),
            pltpu.VMEM((halves, n_col, thin, cols // halves), f32),
            pltpu.VMEM((chunks, 2, n_pair, thin, part), f32),
            pltpu.VMEM((chunks, n_pair, thin, part), f32),
            pltpu.VMEM((chunks, n_pair, thin, part), f32),
            pltpu.VMEM((chunks, n_pair, thin, part), f32),
            pltpu.VMEM((n_col, thin, width), f32),
            pltpu.VMEM((n_col, thin, width), f32),
            pltpu.VMEM((n_row, thin, width), f32),
            dma((4,)),
            dma((2 * n_row * halves,)), dma((n_row * halves,)),
            dma((n_pair,)), dma((n_pair,)),
            dma((n_pair,)), dma((n_pair,)),
            dma((n_col * halves,)), dma((n_col * halves,)),
            dma((chunks,)), dma((chunks,)),
            dma((chunks * n_pair,)), dma((chunks * n_pair,)),
            dma((n_col,)), dma((n_col,)),
            dma((n_row,)), dma((n_row,)),
        ],
        compiler_params=pltpu.CompilerParams(
            collective_id=0, has_side_effects=True, vmem_limit_bytes=60 * 2**20
        ),
    )(panel_index, trail_adjoint, panel.T, panel_adjoint.T, inv_diag)
    return grad.T, diag.T


def choose(trail_adjoint, panel, panel_adjoint, inv_diag, panel_index):
    step = fused if panel.shape[1] % 8 == 0 else body
    return step(trail_adjoint, panel, panel_adjoint, inv_diag, panel_index)


def solution(mesh):
    in_specs = (P("row", "col"), P("row", "col"), P("row", "col"), P(), P())
    out_specs = (P("row", "col"), P(None, "col"))
    return jax.shard_map(choose, mesh=mesh, in_specs=in_specs, out_specs=out_specs, check_vma=False)
```

```python
import functools

import jax
import jax.numpy as jnp
from jax import lax
from jax.experimental import pallas as pl
from jax.experimental.pallas import tpu as pltpu
from jax.sharding import PartitionSpec as P

MESH = pl.DeviceIdType.MESH


def broadcast(value, axis, root):
    mine = lax.axis_index(axis) == root
    return lax.psum(jnp.where(mine, value, jnp.zeros_like(value)), axis)


def body(trail_adjoint, panel, panel_adjoint, inv_diag, panel_index):
    rows_here, thin_cols = panel.shape
    panel_width = inv_diag.shape[0]
    ways_row = lax.axis_size("row")
    ways_col = lax.axis_size("col")
    ways_ratio = ways_col // ways_row
    col_here = lax.axis_index("col")
    index_k = panel_index[0]
    start_mod = jnp.mod(col_here - index_k - 1, ways_col)
    offset = start_mod // ways_row
    col_blocks = rows_here // (panel_width * ways_ratio)
    root_row = jnp.mod(col_here, ways_row)
    panel_rows = lax.all_gather(panel, "col", axis=1, tiled=True)
    shaped = broadcast(panel_rows, "row", root_row).reshape(
        col_blocks, ways_ratio, panel_width, panel_width
    )
    chosen = lax.dynamic_slice_in_dim(shaped, offset, 1, 1)
    column_panel = chosen.reshape(col_blocks * panel_width, panel_width)
    product = jnp.dot(
        trail_adjoint,
        column_panel,
        precision=lax.Precision.HIGHEST,
        preferred_element_type=jnp.float32,
    )
    placed = lax.dynamic_update_slice_in_dim(
        jnp.zeros((rows_here, panel_width), jnp.float32), panel_adjoint, col_here * thin_cols, 1
    )
    local_term = placed - 2.0 * product
    my_inverse = lax.dynamic_slice_in_dim(inv_diag, col_here * thin_cols, thin_cols, 1)
    contract_rows = (((0,), (0,)), ((), ()))
    thin_part = lax.psum_scatter(local_term, "col", scatter_dimension=1, tiled=True)
    full_rows = lax.all_gather(thin_part, "col", axis=1, tiled=True)
    panel_grad = jnp.dot(
        full_rows, my_inverse, precision=lax.Precision.HIGHEST, preferred_element_type=jnp.float32
    )
    gram_local = lax.dot_general(
        full_rows,
        panel,
        contract_rows,
        precision=lax.Precision.HIGHEST,
        preferred_element_type=jnp.float32,
    )
    gram_total = lax.psum(gram_local, "row")
    diag_grad = -lax.dot_general(
        inv_diag,
        gram_total,
        contract_rows,
        precision=lax.Precision.HIGHEST,
        preferred_element_type=jnp.float32,
    )
    return (panel_grad, diag_grad)


CHUNKS = 2


def split(value):
    high = value.astype(jnp.bfloat16)
    return high, (value - high.astype(jnp.float32)).astype(jnp.bfloat16)


def dot(a, b, dims):
    return lax.dot_general(a, b, (dims, ((), ())), preferred_element_type=jnp.float32)


def kernel(
    n_row, n_col, idx_ref, trail_ref, panel_ref, adj_ref, inv_ref, grad_ref, diag_ref,
    trail_v, panel_v, adj_v, inv_v, t_hi, t_lo, base, z_buf, p_full, stage, cp_buf, q_buf, sib_in, q_sum, q_in,
    d_buf, d_in, d_z, loads, z_send, z_recv, p_send, p_recv, f_send, f_recv, c_send, c_recv, s_send, s_recv,
    q_send, q_recv, d_send, d_recv, dz_send, dz_recv,
):
    thin, rows = panel_v.shape
    width = inv_v.shape[0]
    cols = trail_v.shape[1]
    ratio = n_col // n_row
    n_pair = n_col // 2
    chunks = q_sum.shape[0]
    part = rows // chunks
    my_row, my_col = lax.axis_index("row"), lax.axis_index("col")
    my_pair, my_core = my_col // 2, lax.rem(my_col, 2)
    sibling = {"col": my_pair * 2 + 1 - my_core}

    panel_load = pltpu.make_async_copy(panel_ref, panel_v, loads.at[0])
    inv_load = pltpu.make_async_copy(inv_ref, inv_v, loads.at[1])
    adj_load = pltpu.make_async_copy(adj_ref, adj_v, loads.at[2])
    trail_load = pltpu.make_async_copy(trail_ref, trail_v, loads.at[3])
    for load in (panel_load, inv_load, adj_load, trail_load):
        load.start()

    def row_at(shift):
        return {"row": lax.rem(my_row + shift, n_row)}

    def col_at(shift):
        return {"col": lax.rem(my_col + shift, n_col)}

    def col_from(shift):
        return lax.rem(my_col + n_col - shift, n_col)

    def pair_at(shift):
        return lax.rem(my_pair + shift, n_pair)

    def pair_from(shift):
        return lax.rem(my_pair + n_pair - shift, n_pair)

    barrier = pltpu.get_barrier_semaphore()
    for shift in range(1, n_row):
        pl.semaphore_signal(barrier, inc=1, device_id=row_at(shift), device_id_type=MESH)
    for shift in range(1, n_col):
        pl.semaphore_signal(barrier, inc=1, device_id=col_at(shift), device_id_type=MESH)
    panel_load.wait()
    pl.semaphore_wait(barrier, n_row + n_col - 2)

    def remote(src, dst, send, recv, where):
        return pltpu.make_async_remote_copy(
            src_ref=src, dst_ref=dst, send_sem=send, recv_sem=recv, device_id=where, device_id_type=MESH
        )

    z_copies = [remote(panel_v, z_buf.at[s], z_send.at[s], z_recv.at[s], row_at(s)) for s in range(1, n_row)]
    p_copies = [remote(panel_v, p_full.at[my_col], p_send.at[0], p_recv.at[0], sibling)]
    p_copies += [
        remote(
            panel_v, p_full.at[my_col], p_send.at[s], p_recv.at[s], {"col": pair_at(s) * 2 + my_core}
        )
        for s in range(1, n_pair)
    ]
    for copy in z_copies + p_copies:
        copy.start()

    index_k = idx_ref[0]

    def forward(shift):
        piece = panel_v[...] if shift == 0 else z_buf[shift]
        source = lax.rem(my_row + n_row - shift, n_row)
        for group in range(ratio):
            target = source + n_row * group
            offset = jnp.mod(target - index_k - 1, n_col) // n_row
            slot = shift * ratio + group
            for block in range(rows // (width * ratio)):
                at = block * ratio * width
                chosen = piece[:, at : at + width]
                for other in range(1, ratio):
                    chosen = jnp.where(
                        offset == other, piece[:, at + other * width : at + (other + 1) * width], chosen
                    )
                stage[slot, :, block * width : (block + 1) * width] = chosen
            away = lax.rem(target + n_col - my_col, n_col)

            @pl.when(away != 0)
            def _():
                remote(
                    stage.at[slot], cp_buf.at[my_col], c_send.at[away], c_recv.at[away], {"col": target}
                ).start()

            @pl.when(away == 0)
            def _():
                cp_buf[my_col] = stage[slot]

    forward(0)
    p_full[my_col] = panel_v[...]

    trail_load.wait()
    t_high, t_low = split(trail_v[...])
    t_hi[...] = t_high
    t_lo[...] = t_low

    relays = []
    for s in range(1, n_pair):
        slot = p_full.at[pair_from(s) * 2 + my_core]
        remote(slot, slot, p_send.at[s], p_recv.at[s], sibling).wait_recv()
        relay = remote(slot, slot, f_send.at[s], f_recv.at[s], sibling)
        relay.start()
        relays.append(relay)

    adj_load.wait()
    inv_load.wait()
    adj_hi, adj_lo = split(adj_v[...])
    inv_hi, inv_lo = split(inv_v[pl.ds(pl.multiple_of(my_col * thin, 8), thin), :])
    base[...] = dot(
        jnp.concatenate([inv_hi, inv_lo, inv_hi], 0), jnp.concatenate([adj_hi, adj_hi, adj_lo], 0), ((0,), (0,))
    )
    for shift in range(1, n_row):
        z_copies[shift - 1].wait_recv()
        forward(shift)

    p_copies[0].wait_recv()
    for s in range(1, n_pair):
        slot = p_full.at[pair_from(s) * 2 + 1 - my_core]
        remote(slot, slot, f_send.at[s], f_recv.at[s], sibling).wait_recv()
    nt, nn = ((1,), (1,)), ((1,), (0,))
    f_hi, f_lo = split(p_full[...].reshape(width, rows))
    x = dot(jnp.concatenate([f_hi, f_lo], 0), t_hi[...], nn)
    x = x[:width] + x[width:] + dot(f_hi, t_lo[...], nn)
    x_hi, x_lo = split(x)
    b_hi, b_lo = split(base[...])
    d = dot(f_hi, b_hi, nt) + dot(f_hi, b_lo, nt) + dot(f_lo, b_hi, nt)

    inv_hi, inv_lo = split(inv_v[...].T)
    for s in range(1, n_col):
        where = cp_buf.at[col_from(s)]
        remote(where, where, c_send.at[s], c_recv.at[s], col_at(s)).wait_recv()
    cp_hi, cp_lo = split(cp_buf[...].reshape(width, cols))
    w = -2.0 * dot(
        jnp.concatenate([inv_hi, inv_lo, inv_hi], 1), jnp.concatenate([cp_hi, cp_hi, cp_lo], 0), ((1,), (0,))
    )
    w_hi, w_lo = split(w)
    w_both = jnp.concatenate([w_hi, w_lo], 0)

    s_copies, d_copies = [], []
    for h in range(chunks):
        at = slice(h * part, (h + 1) * part)
        both = dot(w_both, t_hi[at, :], nt)
        q = base[:, at] + both[:width] + both[width:] + dot(w_hi, t_lo[at, :], nt)
        by_core = q.reshape(n_pair, 2, thin, part)
        for core in range(2):
            q_buf[h, core] = by_core[:, core]
        copy = remote(q_buf.at[h, 1 - my_core], sib_in.at[h], s_send.at[h], s_recv.at[h], sibling)
        copy.start()
        s_copies.append(copy)
        if h == 0:
            d = -(d + dot(x_hi, w_hi, nt) + dot(x_hi, w_lo, nt) + dot(x_lo, w_hi, nt))
            d_buf[...] = d.reshape(n_col, thin, width)
            for s in range(1, n_col):
                copy = remote(
                    d_buf.at[lax.rem(my_col + s, n_col)], d_in.at[s], d_send.at[s], d_recv.at[s], col_at(s)
                )
                copy.start()
                d_copies.append(copy)

    q_copies = []

    def reduce_out(h):
        s_copies[h].wait_recv()
        q_sum[h] = q_buf[h, my_core] + sib_in[h]
        for s in range(1, n_pair):
            sem = h * n_pair + s
            copy = remote(
                q_sum.at[h, pair_at(s)], q_in.at[h, s], q_send.at[sem], q_recv.at[sem],
                {"col": pair_at(s) * 2 + my_core},
            )
            copy.start()
            q_copies.append(copy)

    for h in range(chunks):
        reduce_out(h)

    total = d_buf[my_col]
    for s in range(1, n_col):
        d_copies[s - 1].wait_recv()
        total = total + d_in[s]
    d_z[my_row] = total
    dz_copies = []
    for s in range(1, n_row):
        copy = remote(d_z.at[my_row], d_z.at[my_row], dz_send.at[s], dz_recv.at[s], row_at(s))
        copy.start()
        dz_copies.append(copy)

    for h in range(chunks):
        total = q_sum[h, my_pair]
        for s in range(1, n_pair):
            q_copies[h * (n_pair - 1) + s - 1].wait_recv()
            total = total + q_in[h, s]
        grad_ref[:, h * part : (h + 1) * part] = total

    for s in range(1, n_row):
        where = d_z.at[lax.rem(my_row + n_row - s, n_row)]
        remote(where, where, dz_send.at[s], dz_recv.at[s], row_at(s)).wait_recv()
    total = d_z[0]
    for r in range(1, n_row):
        total = total + d_z[r]
    diag_ref[...] = total

    for s in range(1, n_col):
        remote(stage.at[0], cp_buf.at[my_col], c_send.at[s], c_recv.at[s], col_at(s)).wait_send()
    for copy in z_copies + p_copies + relays + s_copies + q_copies + d_copies + dz_copies:
        copy.wait_send()


def fused(trail_adjoint, panel, panel_adjoint, inv_diag, panel_index):
    rows, thin = panel.shape
    cols = trail_adjoint.shape[1]
    width = inv_diag.shape[0]
    n_row, n_col = lax.axis_size("row"), lax.axis_size("col")
    n_pair, chunks = n_col // 2, CHUNKS
    part = rows // chunks
    f32, bf16 = jnp.float32, jnp.bfloat16
    vmem, hbm = pl.BlockSpec(memory_space=pltpu.VMEM), pl.BlockSpec(memory_space=pl.ANY)
    dma = pltpu.SemaphoreType.DMA
    grad, diag = pl.pallas_call(
        functools.partial(kernel, n_row, n_col),
        out_shape=(pltpu.VMEM((thin, rows), f32), pltpu.VMEM((thin, width), f32)),
        in_specs=[pl.BlockSpec(memory_space=pltpu.SMEM), hbm, hbm, hbm, hbm],
        out_specs=(vmem, vmem),
        scratch_shapes=[
            pltpu.VMEM((rows, cols), f32),
            pltpu.VMEM((thin, rows), f32),
            pltpu.VMEM((thin, rows), f32),
            pltpu.VMEM((width, width), f32),
            pltpu.VMEM((rows, cols), bf16),
            pltpu.VMEM((rows, cols), bf16),
            pltpu.VMEM((width, rows), f32),
            pltpu.VMEM((n_row, thin, rows), f32),
            pltpu.VMEM((n_col, thin, rows), f32),
            pltpu.VMEM((n_col, thin, cols), f32),
            pltpu.VMEM((n_col, thin, cols), f32),
            pltpu.VMEM((chunks, 2, n_pair, thin, part), f32),
            pltpu.VMEM((chunks, n_pair, thin, part), f32),
            pltpu.VMEM((chunks, n_pair, thin, part), f32),
            pltpu.VMEM((chunks, n_pair, thin, part), f32),
            pltpu.VMEM((n_col, thin, width), f32),
            pltpu.VMEM((n_col, thin, width), f32),
            pltpu.VMEM((n_row, thin, width), f32),
            dma((4,)),
            dma((n_row,)), dma((n_row,)),
            dma((n_pair,)), dma((n_pair,)),
            dma((n_pair,)), dma((n_pair,)),
            dma((n_col,)), dma((n_col,)),
            dma((chunks,)), dma((chunks,)),
            dma((chunks * n_pair,)), dma((chunks * n_pair,)),
            dma((n_col,)), dma((n_col,)),
            dma((n_row,)), dma((n_row,)),
        ],
        compiler_params=pltpu.CompilerParams(
            collective_id=0, has_side_effects=True, vmem_limit_bytes=60 * 2**20
        ),
    )(panel_index, trail_adjoint, panel.T, panel_adjoint.T, inv_diag)
    return grad.T, diag.T


def choose(trail_adjoint, panel, panel_adjoint, inv_diag, panel_index):
    step = fused if panel.shape[1] % 8 == 0 else body
    return step(trail_adjoint, panel, panel_adjoint, inv_diag, panel_index)


def solution(mesh):
    in_specs = (P("row", "col"), P("row", "col"), P("row", "col"), P(), P())
    out_specs = (P("row", "col"), P(None, "col"))
    return jax.shard_map(choose, mesh=mesh, in_specs=in_specs, out_specs=out_specs, check_vma=False)
```
